32 devices in a mesh: outer: 4 (over x, core), dp: 2 (over y), mp: 4 (over z).
Axes of the slice: x: 2, y: 2, z: 4, core: 2. Of those that a mesh axis runs over, the one named last changes fastest.
Arguments:
- inputs: bfloat16 [384, 4096], P('outer', 'dp'), may hold values from -6 to 6
- out_grad: bfloat16 [384, 4096], P('outer', 'dp'), may hold values from -0.59765625 to 0.59765625
- w_gate: bfloat16 [4096, 12288], P('dp', 'mp'), may hold values from -0.09375 to 0.09375
- w_up: bfloat16 [4096, 12288], P('dp', 'mp'), may hold values from -0.09375 to 0.09375
- w_down: bfloat16 [12288, 4096], P('mp', 'dp'), may hold values from -0.0546875 to 0.0546875
Outputs:
- input_grad: bfloat16 [384, 4096], P('outer', 'dp')
- gate_grad: bfloat16 [4096, 12288], P('dp', 'mp')
- up_grad: bfloat16 [4096, 12288], P('dp', 'mp')
- down_grad: bfloat16 [12288, 4096], P('mp', 'dp')
The draws below stay inside these ranges and needn't reach their ends.
All inputs are finite; a program needn't handle non-finite values.
Results may differ from the reference program's by a relative error of at most 0.017.
Values may be sent and summed in bfloat16 or wider, within the bound.
A program may use at most 256 MiB of HBM per device.

```python
import jax
import jax.numpy as jnp
from jax import lax

D = 4096
FF = 12288
TOK_POD = 96
TOKENS = 384
N_OUTER = 4
N_DP = 2


def raised(entries, own_key, source, target, blocks, factor):
    owner, partner = [(jnp.arange(entries.shape[dim]) // (entries.shape[dim] // blocks)).reshape([-1 if axis == dim else 1 for axis in range(entries.ndim)]) for dim in (source, target)]
    chosen = jax.random.permutation(own_key, blocks)[partner]
    strong = (owner == chosen) | (owner == (partner + blocks // 2) % blocks)
    return jnp.where(strong, factor * entries, entries)


def block_scale(own_key, extent, split, least, high):
    def one(dim, parts):
        steps = jax.random.uniform(jax.random.fold_in(jax.random.fold_in(own_key, 6), dim), (parts,), jnp.float32, least / len(split), high / len(split))
        return jnp.repeat(jnp.exp(steps), extent[dim] // parts).reshape((-1,) + (1,) * (len(extent) - dim - 1))

    loudness = one(*split[0])
    for cut in split[1:]:
        loudness = loudness * one(*cut)
    return loudness


def scatter_about(key, dims, spread, most, split=(), held_as=jnp.bfloat16):
    level = block_scale(key, dims, split, -0.22, 0.18) if split else 1.0
    array = jax.random.normal(key, dims, jnp.float32) * spread * level
    return jnp.minimum(jnp.maximum(array, -most), most).astype(held_as)


def noise_with(stream_key, dims, spread, bound, shards, heavy, kind=jnp.bfloat16):
    values = spread * jax.random.normal(stream_key, dims, jnp.float32)
    if shards:
        values = values * block_scale(stream_key, dims, shards, -0.22, 0.18)
    return jnp.clip(raised(values, jax.random.fold_in(stream_key, 3), *heavy), -bound, bound).astype(kind)


def setup_inputs(seed: int = 0) -> dict:
    key_list = jax.random.split(jax.random.key(seed), 6)
    inputs = noise_with(key_list[0], (TOKENS, D), 1.0, 6.0, ((0, 4), (1, 2)), (1, 0, 4, 2.0))
    out_grad = noise_with(key_list[1], (TOKENS, D), 0.1, 0.59765625, ((0, 4), (1, 2)), (1, 0, 4, 2.0))
    w_gate = scatter_about(key_list[2], (D, FF), D ** -0.5, 0.09375, ((0, 2), (1, 4)))
    w_up = scatter_about(key_list[3], (D, FF), D ** -0.5, 0.09375, ((0, 2), (1, 4)))
    w_down = scatter_about(key_list[4], (FF, D), FF ** -0.5, 0.0546875, ((0, 4), (1, 2)))
    return {"inputs": inputs, "out_grad": out_grad, "w_gate": w_gate, "w_up": w_up, "w_down": w_down}


def block_sum(left, right):
    width = left.shape[1] // N_DP

    def step(total, index):
        left_part = lax.dynamic_slice_in_dim(left, index * width, width, 1)
        right_part = lax.dynamic_slice_in_dim(right, index * width, width, 0)
        term = jnp.dot(left_part, right_part, preferred_element_type=jnp.float32).astype(jnp.bfloat16)
        term = lax.optimization_barrier(term)
        return total + term.astype(jnp.float32), None

    start = jnp.zeros((left.shape[0], right.shape[1]), jnp.float32)
    total, unused = lax.scan(step, start, jnp.arange(N_DP, dtype=jnp.int32))
    return total


def pod_sum(left, right):
    total = jnp.zeros((left.shape[1], right.shape[1]), jnp.float32)
    for pod in range(N_OUTER):
        left_part = left[pod * TOK_POD:(pod + 1) * TOK_POD]
        right_part = right[pod * TOK_POD:(pod + 1) * TOK_POD]
        term = lax.dot_general(left_part, right_part, (((0,), (0,)), ((), ())), preferred_element_type=jnp.float32).astype(jnp.bfloat16)
        term = lax.optimization_barrier(term)
        total = total + term.astype(jnp.float32)
    return total.astype(jnp.bfloat16)


def reference(inputs, out_grad, w_gate, w_up, w_down):
    gate = block_sum(inputs, w_gate)
    up = block_sum(inputs, w_up)
    hidden_grad = block_sum(out_grad, jnp.transpose(w_down))
    sig = jax.nn.sigmoid(gate)
    hidden = (gate * sig * up).astype(jnp.bfloat16)
    gate_term = (hidden_grad * up * sig * (1.0 + gate * (1.0 - sig))).astype(jnp.bfloat16)
    up_term = (hidden_grad * gate * sig).astype(jnp.bfloat16)
    down_grad = pod_sum(hidden, out_grad)
    gate_grad = pod_sum(inputs, gate_term)
    up_grad = pod_sum(inputs, up_term)
    contract = (((1,), (1,)), ((), ()))
    input_grad = lax.dot_general(gate_term, w_gate, contract, preferred_element_type=jnp.float32)
    input_grad = input_grad + lax.dot_general(up_term, w_up, contract, preferred_element_type=jnp.float32)
    return input_grad.astype(jnp.bfloat16), gate_grad, up_grad, down_grad
```

```python
import jax
import jax.numpy as jnp
from jax import lax
from jax.sharding import PartitionSpec as P

BF16 = jnp.bfloat16


def mm(left, right, dims):
    return lax.dot_general(left, right, (dims, ((), ())), preferred_element_type=jnp.float32)


def transposed_left(left, right):
    return mm(left, right, ((0,), (0,)))


def transposed_right(left, right):
    return mm(left, right, ((1,), (1,)))


def terms_of(gate, up, hidden_grad):
    sig = jax.nn.sigmoid(gate)
    hidden = (gate * sig * up).astype(BF16)
    gate_term = (hidden_grad * up * sig * (1.0 + gate * (1.0 - sig))).astype(BF16)
    up_term = (hidden_grad * gate * sig).astype(BF16)
    return hidden, gate_term, up_term


def summed_over_dp(partial, dp):
    if dp == 2:
        other = lax.ppermute(partial, "dp", [(0, 1), (1, 0)])
        return partial.astype(jnp.float32) + other.astype(jnp.float32)
    part = lax.psum_scatter(partial, "dp", scatter_dimension=0, tiled=True)
    return lax.all_gather(part, "dp", axis=0, tiled=True).astype(jnp.float32)


def on_device(dp, inputs, out_grad, w_gate, w_up, w_down):
    all_in = lax.all_gather(inputs, "outer", axis=0, tiled=True)
    all_grad = lax.all_gather(out_grad, "outer", axis=0, tiled=True)
    gate = summed_over_dp(mm(inputs, w_gate, ((1,), (0,))).astype(BF16), dp)
    up = summed_over_dp(mm(inputs, w_up, ((1,), (0,))).astype(BF16), dp)
    hidden_grad = summed_over_dp(transposed_right(out_grad, w_down).astype(BF16), dp)
    hidden, gate_term, up_term = terms_of(gate, up, hidden_grad)
    all_hidden = lax.all_gather(hidden, "outer", axis=0, tiled=True)
    all_up = lax.all_gather(up_term, "outer", axis=0, tiled=True)
    all_gate = lax.all_gather(gate_term, "outer", axis=0, tiled=True)
    rows_back = transposed_right(gate_term, w_gate) + transposed_right(up_term, w_up)
    input_grad = lax.psum(rows_back.astype(BF16), "mp")
    down_grad = transposed_left(all_hidden, all_grad).astype(BF16)
    up_grad = transposed_left(all_in, all_up).astype(BF16)
    gate_grad = transposed_left(all_in, all_gate).astype(BF16)
    return input_grad, gate_grad, up_grad, down_grad


def solution(mesh):
    dp = mesh.shape["dp"]
    in_specs = (P("outer", "dp"), P("outer", "dp"), P("dp", "mp"), P("dp", "mp"), P("mp", "dp"))
    out_specs = (P("outer", "dp"), P("dp", "mp"), P("dp", "mp"), P("mp", "dp"))

    def body(*arrays):
        return on_device(dp, *arrays)

    return jax.shard_map(body, mesh=mesh, in_specs=in_specs, out_specs=out_specs, check_vma=False)
```

```python
import functools

import jax
import jax.numpy as jnp
from jax import lax
from jax.experimental import pallas as pl
from jax.experimental.pallas import tpu as pltpu
from jax.sharding import PartitionSpec as P

BF16 = jnp.bfloat16


def mm(left, right, dims):
    return lax.dot_general(left, right, (dims, ((), ())), preferred_element_type=jnp.float32)


def transposed_left(left, right):
    return mm(left, right, ((0,), (0,)))


def transposed_right(left, right):
    return mm(left, right, ((1,), (1,)))


def terms_of(gate, up, hidden_grad):
    sig = jax.nn.sigmoid(gate)
    hidden = (gate * sig * up).astype(BF16)
    gate_term = (hidden_grad * up * sig * (1.0 + gate * (1.0 - sig))).astype(BF16)
    up_term = (hidden_grad * gate * sig).astype(BF16)
    return hidden, gate_term, up_term


def summed_over_dp(partial, dp):
    if dp == 2:
        other = lax.ppermute(partial, "dp", [(0, 1), (1, 0)])
        return partial.astype(jnp.float32) + other.astype(jnp.float32)
    part = lax.psum_scatter(partial, "dp", scatter_dimension=0, tiled=True)
    return lax.all_gather(part, "dp", axis=0, tiled=True).astype(jnp.float32)


def on_device(dp, inputs, out_grad, w_gate, w_up, w_down):
    all_in = lax.all_gather(inputs, "outer", axis=0, tiled=True)
    all_grad = lax.all_gather(out_grad, "outer", axis=0, tiled=True)
    gate = summed_over_dp(mm(inputs, w_gate, ((1,), (0,))).astype(BF16), dp)
    up = summed_over_dp(mm(inputs, w_up, ((1,), (0,))).astype(BF16), dp)
    hidden_grad = summed_over_dp(transposed_right(out_grad, w_down).astype(BF16), dp)
    hidden, gate_term, up_term = terms_of(gate, up, hidden_grad)
    all_hidden = lax.all_gather(hidden, "outer", axis=0, tiled=True)
    all_up = lax.all_gather(up_term, "outer", axis=0, tiled=True)
    all_gate = lax.all_gather(gate_term, "outer", axis=0, tiled=True)
    rows_back = transposed_right(gate_term, w_gate) + transposed_right(up_term, w_up)
    input_grad = lax.psum(rows_back.astype(BF16), "mp")
    down_grad = transposed_left(all_hidden, all_grad).astype(BF16)
    up_grad = transposed_left(all_in, all_up).astype(BF16)
    gate_grad = transposed_left(all_in, all_gate).astype(BF16)
    return input_grad, gate_grad, up_grad, down_grad


MESH = pl.DeviceIdType.MESH
CHUNK = 512
LAG = 2


def exchange_kernel(
    chunks, x_ref, g_ref, x_any, g_any, wg_any, wu_any, wd_any,
    all_x, all_g, terms, back,
    wg, wu, wd, partial, other, mine, acc,
    w_sem, y_send, y_recv, x_send, x_recv, c_send, c_recv, f_send, f_recv, own_sem,
):
    me = lax.axis_index("outer")
    across = lax.rem(me + 2, 4)
    sibling = me + 1 - 2 * lax.rem(me, 2)
    width = lax.rem(lax.axis_index("dp") + 1, 2)
    loads = ((wg_any, wg), (wu_any, wu), (wd_any, wd))

    def columns(c):
        return pl.ds(pl.multiple_of(c * CHUNK, CHUNK), CHUNK)

    def load(c, k):
        source, target = loads[k]
        piece = source.at[columns(c), :] if k == 2 else source.at[:, columns(c)]
        return pltpu.make_async_copy(piece, target.at[c], w_sem.at[k, c])

    def start_loads(c, carry):
        for k in range(3):
            load(c, k).start()
        return carry

    lax.fori_loop(0, chunks, start_loads, 0)

    barrier = pltpu.get_barrier_semaphore()
    pl.semaphore_signal(barrier, inc=1, device_id={"outer": across}, device_id_type=MESH)
    pl.semaphore_signal(barrier, inc=1, device_id={"outer": sibling}, device_id_type=MESH)
    pl.semaphore_signal(barrier, inc=1, device_id={"dp": width}, device_id_type=MESH)
    pl.semaphore_wait(barrier, 3)

    def remote(source, target, send, recv, axis, peer):
        return pltpu.make_async_remote_copy(
            src_ref=source, dst_ref=target, send_sem=send, recv_sem=recv,
            device_id={axis: peer}, device_id_type=MESH,
        )

    def act(i):
        return (x_any, all_x) if i == 0 else (g_any, all_g)

    def act_copies(i):
        source, target = act(i)
        place = target.at[me]
        return (
            remote(source, place, x_send.at[i], x_recv.at[i], "outer", across),
            remote(source, place, c_send.at[i], c_recv.at[i], "outer", sibling),
            pltpu.make_async_copy(source, place, own_sem.at[i]),
        )

    def term_copies(c):
        source = mine.at[c]
        place = terms.at[:, me, :, columns(c)]
        i = c + 2
        return (
            remote(source, place, x_send.at[i], x_recv.at[i], "outer", across),
            remote(source, place, c_send.at[i], c_recv.at[i], "outer", sibling),
            pltpu.make_async_copy(source, place, own_sem.at[i]),
        )

    def act_forward(i):
        place = act(i)[1].at[across]
        return remote(place, place, f_send.at[i], f_recv.at[i], "outer", sibling)

    def term_forward(c):
        place = terms.at[:, across, :, columns(c)]
        return remote(place, place, f_send.at[c + 2], f_recv.at[c + 2], "outer", sibling)

    def y_copy(c):
        return remote(partial.at[c], other.at[c], y_send.at[c], y_recv.at[c], "dp", width)

    for i in range(2):
        for copy in act_copies(i):
            copy.start()
    acc[...] = jnp.zeros_like(acc)

    def step(s, carry):
        @pl.when(s < chunks)
        def _():
            for k in range(3):
                load(s, k).wait()
            x = x_ref[...]
            partial[s, 0] = mm(x, wg[s], ((1,), (0,))).astype(BF16)
            partial[s, 1] = mm(x, wu[s], ((1,), (0,))).astype(BF16)
            partial[s, 2] = mm(g_ref[...], wd[s], ((1,), (1,))).astype(BF16)
            y_copy(s).start()

        @pl.when(s >= LAG)
        def _():
            c = s - LAG
            y_copy(c).wait_recv()
            gate, up, hidden_grad = [
                partial[c, k].astype(jnp.float32) + other[c, k].astype(jnp.float32) for k in range(3)
            ]
            hidden, gate_term, up_term = terms_of(gate, up, hidden_grad)
            mine[c, 0] = hidden
            mine[c, 1] = gate_term
            mine[c, 2] = up_term
            for copy in term_copies(c):
                copy.start()
            acc[...] += mm(gate_term, wg[c], ((1,), (1,))) + mm(up_term, wu[c], ((1,), (1,)))

        return carry

    lax.fori_loop(0, chunks + LAG, step, 0)
    back[...] = acc[...].astype(BF16)

    for i in range(2):
        act_copies(i)[0].wait_recv()
        act_forward(i).start()

    def forward(c, carry):
        term_copies(c)[0].wait_recv()
        term_forward(c).start()
        return carry

    lax.fori_loop(0, chunks, forward, 0)

    def finish(copies, passed):
        copies[0].wait_send()
        copies[1].wait()
        copies[2].wait()
        passed.wait()

    for i in range(2):
        finish(act_copies(i), act_forward(i))

    def drain(c, carry):
        y_copy(c).wait_send()
        finish(term_copies(c), term_forward(c))
        return carry

    lax.fori_loop(0, chunks, drain, 0)


def exchange(inputs, out_grad, w_gate, w_up, w_down):
    rows, width = inputs.shape
    hidden = w_gate.shape[1]
    chunks = hidden // CHUNK
    any_spec = pl.BlockSpec(memory_space=pl.ANY)
    vmem_spec = pl.BlockSpec(memory_space=pltpu.VMEM)
    dma = pltpu.SemaphoreType.DMA
    items = dma((chunks + 2,))
    return pl.pallas_call(
        functools.partial(exchange_kernel, chunks),
        out_shape=(
            jax.ShapeDtypeStruct((4, rows, width), BF16),
            jax.ShapeDtypeStruct((4, rows, width), BF16),
            jax.ShapeDtypeStruct((3, 4, rows, hidden), BF16),
            jax.ShapeDtypeStruct((rows, width), BF16),
        ),
        in_specs=[vmem_spec] * 2 + [any_spec] * 5,
        out_specs=(any_spec, any_spec, any_spec, vmem_spec),
        scratch_shapes=[
            pltpu.VMEM((chunks, width, CHUNK), BF16),
            pltpu.VMEM((chunks, width, CHUNK), BF16),
            pltpu.VMEM((chunks, CHUNK, width), BF16),
            pltpu.VMEM((chunks, 3, rows, CHUNK), BF16),
            pltpu.VMEM((chunks, 3, rows, CHUNK), BF16),
            pltpu.VMEM((chunks, 3, rows, CHUNK), BF16),
            pltpu.VMEM((rows, width), jnp.float32),
            dma((3, chunks)), dma((chunks,)), dma((chunks,)),
            items, items, items, items, items, items, items,
        ],
        compiler_params=pltpu.CompilerParams(
            collective_id=0, has_side_effects=True, vmem_limit_bytes=56 * 1024 * 1024
        ),
    )(inputs, out_grad, inputs, out_grad, w_gate, w_up, w_down)


PARTS = 8


def grads_kernel(x_ref, g_ref, h_ref, gt_ref, ut_ref, gate_out, up_out, down_out):
    left = x_ref[...].T
    for start in range(0, gate_out.shape[1], 1024):
        cut = slice(start, start + 1024)
        gate_out[:, cut] = jnp.dot(left, gt_ref[0, :, cut], preferred_element_type=jnp.float32).astype(BF16)
        up_out[:, cut] = jnp.dot(left, ut_ref[0, :, cut], preferred_element_type=jnp.float32).astype(BF16)
    left = h_ref[0].T
    for start in range(0, down_out.shape[1], 1024):
        cut = slice(start, start + 1024)
        down_out[:, cut] = jnp.dot(left, g_ref[:, cut], preferred_element_type=jnp.float32).astype(BF16)


def weight_grads(all_x, all_g, terms):
    tokens, width = all_x.shape
    hidden = terms.shape[2]
    cost = pl.CostEstimate(
        flops=6 * tokens * width * hidden,
        bytes_accessed=2 * (3 * width * hidden + tokens * (2 * width + 3 * hidden)),
        transcendentals=0,
    )
    return pl.pallas_call(
        grads_kernel,
        grid=(PARTS,),
        out_shape=(
            jax.ShapeDtypeStruct((width, hidden), BF16),
            jax.ShapeDtypeStruct((width, hidden), BF16),
            jax.ShapeDtypeStruct((hidden, width), BF16),
        ),
        in_specs=[
            pl.BlockSpec((tokens, width // PARTS), lambda i: (0, i)),
            pl.BlockSpec((tokens, width), lambda i: (0, 0)),
            pl.BlockSpec((1, tokens, hidden // PARTS), lambda i: (0, 0, i)),
            pl.BlockSpec((1, tokens, hidden), lambda i: (1, 0, 0)),
            pl.BlockSpec((1, tokens, hidden), lambda i: (2, 0, 0)),
        ],
        out_specs=(
            pl.BlockSpec((width // PARTS, hidden), lambda i: (i, 0)),
            pl.BlockSpec((width // PARTS, hidden), lambda i: (i, 0)),
            pl.BlockSpec((hidden // PARTS, width), lambda i: (i, 0)),
        ),
        compiler_params=pltpu.CompilerParams(vmem_limit_bytes=48 * 1024 * 1024),
        cost_estimate=cost,
    )(all_x, all_g, terms, terms, terms)


def on_device_kernels(inputs, out_grad, w_gate, w_up, w_down):
    all_x, all_g, terms, back = exchange(inputs, out_grad, w_gate, w_up, w_down)
    input_grad = lax.psum(back, "mp")
    rows, width = inputs.shape
    hidden = w_gate.shape[1]
    gate_grad, up_grad, down_grad = weight_grads(
        all_x.reshape(4 * rows, width), all_g.reshape(4 * rows, width), terms.reshape(3, 4 * rows, hidden)
    )
    return input_grad, gate_grad, up_grad, down_grad


def solution(mesh):
    dp = mesh.shape["dp"]
    in_specs = (P("outer", "dp"), P("outer", "dp"), P("dp", "mp"), P("dp", "mp"), P("mp", "dp"))
    out_specs = (P("outer", "dp"), P("dp", "mp"), P("dp", "mp"), P("mp", "dp"))

    def body(*arrays):
        rows, width = arrays[0].shape
        hidden = arrays[2].shape[1]
        fits = rows % 16 == 0 and 6 * width * hidden <= 40 * 1024 * 1024
        tiles = width % 1024 == 0 and hidden % 1024 == 0
        if dp == 2 and mesh.shape["outer"] == 4 and fits and tiles:
            return on_device_kernels(*arrays)
        return on_device(dp, *arrays)

    return jax.shard_map(body, mesh=mesh, in_specs=in_specs, out_specs=out_specs, check_vma=False)
```

```python
import functools

import jax
import jax.numpy as jnp
from jax import lax
from jax.experimental import pallas as pl
from jax.experimental.pallas import tpu as pltpu
from jax.sharding import PartitionSpec as P

BF16 = jnp.bfloat16


def mm(left, right, dims):
    return lax.dot_general(left, right, (dims, ((), ())), preferred_element_type=jnp.float32)


def transposed_left(left, right):
    return mm(left, right, ((0,), (0,)))


def transposed_right(left, right):
    return mm(left, right, ((1,), (1,)))


def terms_of(gate, up, hidden_grad):
    sig = jax.nn.sigmoid(gate)
    hidden = (gate * sig * up).astype(BF16)
    gate_term = (hidden_grad * up * sig * (1.0 + gate * (1.0 - sig))).astype(BF16)
    up_term = (hidden_grad * gate * sig).astype(BF16)
    return hidden, gate_term, up_term


def summed_over_dp(partial, dp):
    if dp == 2:
        other = lax.ppermute(partial, "dp", [(0, 1), (1, 0)])
        return partial.astype(jnp.float32) + other.astype(jnp.float32)
    part = lax.psum_scatter(partial, "dp", scatter_dimension=0, tiled=True)
    return lax.all_gather(part, "dp", axis=0, tiled=True).astype(jnp.float32)


def on_device(dp, inputs, out_grad, w_gate, w_up, w_down):
    all_in = lax.all_gather(inputs, "outer", axis=0, tiled=True)
    all_grad = lax.all_gather(out_grad, "outer", axis=0, tiled=True)
    gate = summed_over_dp(mm(inputs, w_gate, ((1,), (0,))).astype(BF16), dp)
    up = summed_over_dp(mm(inputs, w_up, ((1,), (0,))).astype(BF16), dp)
    hidden_grad = summed_over_dp(transposed_right(out_grad, w_down).astype(BF16), dp)
    hidden, gate_term, up_term = terms_of(gate, up, hidden_grad)
    all_hidden = lax.all_gather(hidden, "outer", axis=0, tiled=True)
    all_up = lax.all_gather(up_term, "outer", axis=0, tiled=True)
    all_gate = lax.all_gather(gate_term, "outer", axis=0, tiled=True)
    rows_back = transposed_right(gate_term, w_gate) + transposed_right(up_term, w_up)
    input_grad = lax.psum(rows_back.astype(BF16), "mp")
    down_grad = transposed_left(all_hidden, all_grad).astype(BF16)
    up_grad = transposed_left(all_in, all_up).astype(BF16)
    gate_grad = transposed_left(all_in, all_gate).astype(BF16)
    return input_grad, gate_grad, up_grad, down_grad


MESH = pl.DeviceIdType.MESH
CHUNK = 512
LAG = 2


def exchange_kernel(
    chunks, x_ref, g_ref, x_any, g_any, wg_any, wu_any, wd_any,
    all_x, all_g, terms, back,
    wg, wu, wd, partial, other, mine, acc, back_out, back_in, back_all,
    w_sem, y_send, y_recv, x_send, x_recv, c_send, c_recv, f_send, f_recv, own_sem,
    z_send, z_recv, s_send, s_recv, g_send, g_recv,
):
    me = lax.axis_index("outer")
    across = lax.rem(me + 2, 4)
    sibling = me + 1 - 2 * lax.rem(me, 2)
    width = lax.rem(lax.axis_index("dp") + 1, 2)
    level = lax.axis_index("mp")
    levels = back_all.shape[0]
    quarter = back_all.shape[2]
    own_cut = pl.ds(pl.multiple_of(level * quarter, quarter), quarter)

    def above(d):
        return lax.rem(level + d, levels)

    loads = ((wg_any, wg), (wu_any, wu), (wd_any, wd))

    def columns(c):
        return pl.ds(pl.multiple_of(c * CHUNK, CHUNK), CHUNK)

    def load(c, k):
        source, target = loads[k]
        piece = source.at[columns(c), :] if k == 2 else source.at[:, columns(c)]
        return pltpu.make_async_copy(piece, target.at[c], w_sem.at[k, c])

    def start_loads(c, carry):
        for k in range(3):
            load(c, k).start()
        return carry

    lax.fori_loop(0, chunks, start_loads, 0)

    barrier = pltpu.get_barrier_semaphore()
    pl.semaphore_signal(barrier, inc=1, device_id={"outer": across}, device_id_type=MESH)
    pl.semaphore_signal(barrier, inc=1, device_id={"outer": sibling}, device_id_type=MESH)
    pl.semaphore_signal(barrier, inc=1, device_id={"dp": width}, device_id_type=MESH)
    for d in range(1, levels):
        pl.semaphore_signal(barrier, inc=1, device_id={"mp": above(d)}, device_id_type=MESH)
    pl.semaphore_wait(barrier, 2 + levels)

    def remote(source, target, send, recv, axis, peer):
        return pltpu.make_async_remote_copy(
            src_ref=source, dst_ref=target, send_sem=send, recv_sem=recv,
            device_id={axis: peer}, device_id_type=MESH,
        )

    def act(i):
        return (x_any, all_x) if i == 0 else (g_any, all_g)

    def act_copies(i):
        source, target = act(i)
        place = target.at[me]
        return (
            remote(
                source.at[:, own_cut], target.at[me, :, own_cut],
                x_send.at[i], x_recv.at[i], "outer", across,
            ),
            remote(source, place, c_send.at[i], c_recv.at[i], "outer", sibling),
            pltpu.make_async_copy(source, place, own_sem.at[i]),
        )

    def term_copies(c):
        source = mine.at[c]
        place = terms.at[:, me, :, columns(c)]
        i = c + 2
        return (
            remote(source, place, x_send.at[i], x_recv.at[i], "outer", across),
            remote(source, place, c_send.at[i], c_recv.at[i], "outer", sibling),
            pltpu.make_async_copy(source, place, own_sem.at[i]),
        )

    def act_spread(i, d):
        place = act(i)[1].at[across, :, own_cut]
        return remote(place, place, z_send.at[i, d - 1], z_recv.at[i, d - 1], "mp", above(d))

    def act_forward(i):
        place = act(i)[1].at[across]
        return remote(place, place, f_send.at[i], f_recv.at[i], "outer", sibling)

    def term_forward(c):
        place = terms.at[:, across, :, columns(c)]
        return remote(place, place, f_send.at[c + 2], f_recv.at[c + 2], "outer", sibling)

    def back_scatter(d):
        return remote(
            back_out.at[above(d)], back_in.at[d - 1], s_send.at[d - 1], s_recv.at[d - 1], "mp", above(d)
        )

    def back_gather(d):
        place = back_all.at[level]
        return remote(place, place, g_send.at[d - 1], g_recv.at[d - 1], "mp", above(d))

    def y_copy(c):
        return remote(partial.at[c], other.at[c], y_send.at[c], y_recv.at[c], "dp", width)

    for i in range(2):
        for copy in act_copies(i):
            copy.start()
    acc[...] = jnp.zeros_like(acc)

    def step(s, carry):
        @pl.when(s < chunks)
        def _():
            for k in range(3):
                load(s, k).wait()
            x = x_ref[...]
            partial[s, 0] = mm(x, wg[s], ((1,), (0,))).astype(BF16)
            partial[s, 1] = mm(x, wu[s], ((1,), (0,))).astype(BF16)
            partial[s, 2] = mm(g_ref[...], wd[s], ((1,), (1,))).astype(BF16)
            y_copy(s).start()

        @pl.when(s >= LAG)
        def _():
            c = s - LAG
            y_copy(c).wait_recv()
            gate, up, hidden_grad = [
                partial[c, k].astype(jnp.float32) + other[c, k].astype(jnp.float32) for k in range(3)
            ]
            hidden, gate_term, up_term = terms_of(gate, up, hidden_grad)
            mine[c, 0] = hidden
            mine[c, 1] = gate_term
            mine[c, 2] = up_term
            for copy in term_copies(c):
                copy.start()
            acc[...] += mm(gate_term, wg[c], ((1,), (1,))) + mm(up_term, wu[c], ((1,), (1,)))

        @pl.when(s == 2)
        def _():
            for i in range(2):
                act_copies(i)[0].wait_recv()
                for d in range(1, levels):
                    act_spread(i, d).start()

        return carry

    lax.fori_loop(0, chunks + LAG, step, 0)
    for j in range(levels):
        back_out[j] = acc[:, j * quarter:(j + 1) * quarter].astype(BF16)
    for d in range(1, levels):
        back_scatter(d).start()

    for i in range(2):
        for d in range(1, levels):
            act_spread(i, d).wait_recv()
        act_forward(i).start()

    def forward(c, carry):
        term_copies(c)[0].wait_recv()
        term_forward(c).start()
        return carry

    lax.fori_loop(0, chunks - 1, forward, 0)

    total = back_out[level].astype(jnp.float32)
    for d in range(1, levels):
        back_scatter(d).wait_recv()
        total = total + back_in[d - 1].astype(jnp.float32)
    back_all[level] = total.astype(BF16)
    for d in range(1, levels):
        back_gather(d).start()

    forward(chunks - 1, 0)

    for d in range(1, levels):
        back_gather(d).wait_recv()
    for j in range(levels):
        back[:, j * quarter:(j + 1) * quarter] = back_all[j]
    for d in range(1, levels):
        back_scatter(d).wait_send()
        back_gather(d).wait_send()

    def finish(copies, passed):
        copies[0].wait_send()
        copies[1].wait()
        copies[2].wait()
        passed.wait()

    for i in range(2):
        finish(act_copies(i), act_forward(i))
        for d in range(1, levels):
            act_spread(i, d).wait_send()

    def drain(c, carry):
        y_copy(c).wait_send()
        finish(term_copies(c), term_forward(c))
        return carry

    lax.fori_loop(0, chunks, drain, 0)


def exchange(levels, inputs, out_grad, w_gate, w_up, w_down):
    rows, width = inputs.shape
    quarter = width // levels
    hidden = w_gate.shape[1]
    chunks = hidden // CHUNK
    any_spec = pl.BlockSpec(memory_space=pl.ANY)
    vmem_spec = pl.BlockSpec(memory_space=pltpu.VMEM)
    dma = pltpu.SemaphoreType.DMA
    items = dma((chunks + 2,))
    return pl.pallas_call(
        functools.partial(exchange_kernel, chunks),
        out_shape=(
            jax.ShapeDtypeStruct((4, rows, width), BF16),
            jax.ShapeDtypeStruct((4, rows, width), BF16),
            jax.ShapeDtypeStruct((3, 4, rows, hidden), BF16),
            jax.ShapeDtypeStruct((rows, width), BF16),
        ),
        in_specs=[vmem_spec] * 2 + [any_spec] * 5,
        out_specs=(any_spec, any_spec, any_spec, vmem_spec),
        scratch_shapes=[
            pltpu.VMEM((chunks, width, CHUNK), BF16),
            pltpu.VMEM((chunks, width, CHUNK), BF16),
            pltpu.VMEM((chunks, CHUNK, width), BF16),
            pltpu.VMEM((chunks, 3, rows, CHUNK), BF16),
            pltpu.VMEM((chunks, 3, rows, CHUNK), BF16),
            pltpu.VMEM((chunks, 3, rows, CHUNK), BF16),
            pltpu.VMEM((rows, width), jnp.float32),
            pltpu.VMEM((levels, rows, quarter), BF16),
            pltpu.VMEM((levels - 1, rows, quarter), BF16),
            pltpu.VMEM((levels, rows, quarter), BF16),
            dma((3, chunks)), dma((chunks,)), dma((chunks,)),
            items, items, items, items, items, items, items,
            dma((2, levels - 1)), dma((2, levels - 1)),
            dma((levels - 1,)), dma((levels - 1,)), dma((levels - 1,)), dma((levels - 1,)),
        ],
        compiler_params=pltpu.CompilerParams(
            collective_id=0, has_side_effects=True, vmem_limit_bytes=60 * 1024 * 1024
        ),
    )(inputs, out_grad, inputs, out_grad, w_gate, w_up, w_down)


PARTS = 8


def grads_kernel(x_ref, g_ref, h_ref, gt_ref, ut_ref, back_ref, gate_out, up_out, down_out, back_out):
    @pl.when(pl.program_id(0) == 0)
    def _():
        back_out[...] = back_ref[...]

    left = x_ref[...].T
    for start in range(0, gate_out.shape[1], 1024):
        cut = slice(start, start + 1024)
        gate_out[:, cut] = jnp.dot(left, gt_ref[0, :, cut], preferred_element_type=jnp.float32).astype(BF16)
        up_out[:, cut] = jnp.dot(left, ut_ref[0, :, cut], preferred_element_type=jnp.float32).astype(BF16)
    left = h_ref[0].T
    for start in range(0, down_out.shape[1], 1024):
        cut = slice(start, start + 1024)
        down_out[:, cut] = jnp.dot(left, g_ref[:, cut], preferred_element_type=jnp.float32).astype(BF16)


def weight_grads(all_x, all_g, terms, back):
    tokens, width = all_x.shape
    hidden = terms.shape[2]
    cost = pl.CostEstimate(
        flops=6 * tokens * width * hidden,
        bytes_accessed=2 * (3 * width * hidden + tokens * (2 * width + 3 * hidden)),
        transcendentals=0,
    )
    return pl.pallas_call(
        grads_kernel,
        grid=(PARTS,),
        out_shape=(
            jax.ShapeDtypeStruct((width, hidden), BF16),
            jax.ShapeDtypeStruct((width, hidden), BF16),
            jax.ShapeDtypeStruct((hidden, width), BF16),
            jax.ShapeDtypeStruct(back.shape, BF16),
        ),
        in_specs=[
            pl.BlockSpec((tokens, width // PARTS), lambda i: (0, i)),
            pl.BlockSpec((tokens, width), lambda i: (0, 0)),
            pl.BlockSpec((1, tokens, hidden // PARTS), lambda i: (0, 0, i)),
            pl.BlockSpec((1, tokens, hidden), lambda i: (1, 0, 0)),
            pl.BlockSpec((1, tokens, hidden), lambda i: (2, 0, 0)),
            pl.BlockSpec(back.shape, lambda i: (0, 0)),
        ],
        out_specs=(
            pl.BlockSpec((width // PARTS, hidden), lambda i: (i, 0)),
            pl.BlockSpec((width // PARTS, hidden), lambda i: (i, 0)),
            pl.BlockSpec((hidden // PARTS, width), lambda i: (i, 0)),
            pl.BlockSpec(back.shape, lambda i: (0, 0)),
        ),
        compiler_params=pltpu.CompilerParams(vmem_limit_bytes=60 * 1024 * 1024),
        cost_estimate=cost,
    )(all_x, all_g, terms, terms, terms, back)


def on_device_kernels(levels, inputs, out_grad, w_gate, w_up, w_down):
    all_x, all_g, terms, back = exchange(levels, inputs, out_grad, w_gate, w_up, w_down)
    rows, width = inputs.shape
    hidden = w_gate.shape[1]
    gate_grad, up_grad, down_grad, input_grad = weight_grads(
        all_x.reshape(4 * rows, width), all_g.reshape(4 * rows, width), terms.reshape(3, 4 * rows, hidden), back
    )
    return input_grad, gate_grad, up_grad, down_grad


def solution(mesh):
    dp = mesh.shape["dp"]
    in_specs = (P("outer", "dp"), P("outer", "dp"), P("dp", "mp"), P("dp", "mp"), P("mp", "dp"))
    out_specs = (P("outer", "dp"), P("dp", "mp"), P("dp", "mp"), P("mp", "dp"))

    def body(*arrays):
        rows, width = arrays[0].shape
        hidden = arrays[2].shape[1]
        fits = rows % 16 == 0 and 6 * width * hidden <= 40 * 1024 * 1024
        tiles = width % 1024 == 0 and hidden % 1024 == 0
        if dp == 2 and mesh.shape["outer"] == 4 and mesh.shape["mp"] == 4 and fits and tiles:
            return on_device_kernels(mesh.shape["mp"], *arrays)
        return on_device(dp, *arrays)

    return jax.shard_map(body, mesh=mesh, in_specs=in_specs, out_specs=out_specs, check_vma=False)
```

```python
import functools

import jax
import jax.numpy as jnp
from jax import lax
from jax.experimental import pallas as pl
from jax.experimental.pallas import tpu as pltpu
from jax.sharding import PartitionSpec as P

BF16 = jnp.bfloat16


def mm(left, right, dims):
    return lax.dot_general(left, right, (dims, ((), ())), preferred_element_type=jnp.float32)


def transposed_left(left, right):
    return mm(left, right, ((0,), (0,)))


def transposed_right(left, right):
    return mm(left, right, ((1,), (1,)))


def terms_of(gate, up, hidden_grad):
    sig = jax.nn.sigmoid(gate)
    hidden = (gate * sig * up).astype(BF16)
    gate_term = (hidden_grad * up * sig * (1.0 + gate * (1.0 - sig))).astype(BF16)
    up_term = (hidden_grad * gate * sig).astype(BF16)
    return hidden, gate_term, up_term


def summed_over_dp(partial, dp):
    if dp == 2:
        other = lax.ppermute(partial, "dp", [(0, 1), (1, 0)])
        return partial.astype(jnp.float32) + other.astype(jnp.float32)
    part = lax.psum_scatter(partial, "dp", scatter_dimension=0, tiled=True)
    return lax.all_gather(part, "dp", axis=0, tiled=True).astype(jnp.float32)


def on_device(dp, inputs, out_grad, w_gate, w_up, w_down):
    all_in = lax.all_gather(inputs, "outer", axis=0, tiled=True)
    all_grad = lax.all_gather(out_grad, "outer", axis=0, tiled=True)
    gate = summed_over_dp(mm(inputs, w_gate, ((1,), (0,))).astype(BF16), dp)
    up = summed_over_dp(mm(inputs, w_up, ((1,), (0,))).astype(BF16), dp)
    hidden_grad = summed_over_dp(transposed_right(out_grad, w_down).astype(BF16), dp)
    hidden, gate_term, up_term = terms_of(gate, up, hidden_grad)
    all_hidden = lax.all_gather(hidden, "outer", axis=0, tiled=True)
    all_up = lax.all_gather(up_term, "outer", axis=0, tiled=True)
    all_gate = lax.all_gather(gate_term, "outer", axis=0, tiled=True)
    rows_back = transposed_right(gate_term, w_gate) + transposed_right(up_term, w_up)
    input_grad = lax.psum(rows_back.astype(BF16), "mp")
    down_grad = transposed_left(all_hidden, all_grad).astype(BF16)
    up_grad = transposed_left(all_in, all_up).astype(BF16)
    gate_grad = transposed_left(all_in, all_gate).astype(BF16)
    return input_grad, gate_grad, up_grad, down_grad


MESH = pl.DeviceIdType.MESH
CHUNK = 256
LAG = 2
AHEAD = 4


def exchange_kernel(
    chunks, x_ref, g_ref, x_any, g_any, wg_any, wu_any, wd_any,
    all_x, all_g, terms, back,
    wg, wu, wd, partial, other, mine, acc, back_out, back_in, back_all,
    w_sem, y_send, y_recv, x_send, x_recv, c_send, c_recv, f_send, f_recv, own_sem,
    z_send, z_recv, s_send, s_recv, g_send, g_recv,
):
    me = lax.axis_index("outer")
    across = lax.rem(me + 2, 4)
    sibling = me + 1 - 2 * lax.rem(me, 2)
    width = lax.rem(lax.axis_index("dp") + 1, 2)
    level = lax.axis_index("mp")
    levels = back_all.shape[0]
    quarter = back_all.shape[2]
    own_cut = pl.ds(pl.multiple_of(level * quarter, quarter), quarter)

    def above(d):
        return lax.rem(level + d, levels)

    loads = ((wg_any, wg), (wu_any, wu), (wd_any, wd))

    def columns(c):
        return pl.ds(pl.multiple_of(c * CHUNK, CHUNK), CHUNK)

    def load(c, k):
        source, target = loads[k]
        piece = source.at[columns(c), :] if k == 2 else source.at[:, columns(c)]
        return pltpu.make_async_copy(piece, target.at[c], w_sem.at[k, c])

    def start_loads(c, carry):
        for k in range(3):
            load(c, k).start()
        return carry

    lax.fori_loop(0, AHEAD, start_loads, 0)

    barrier = pltpu.get_barrier_semaphore()
    pl.semaphore_signal(barrier, inc=1, device_id={"outer": across}, device_id_type=MESH)
    pl.semaphore_signal(barrier, inc=1, device_id={"outer": sibling}, device_id_type=MESH)
    pl.semaphore_signal(barrier, inc=1, device_id={"dp": width}, device_id_type=MESH)
    for d in range(1, levels):
        pl.semaphore_signal(barrier, inc=1, device_id={"mp": above(d)}, device_id_type=MESH)
    pl.semaphore_wait(barrier, 2 + levels)

    def remote(source, target, send, recv, axis, peer):
        return pltpu.make_async_remote_copy(
            src_ref=source, dst_ref=target, send_sem=send, recv_sem=recv,
            device_id={axis: peer}, device_id_type=MESH,
        )

    def act(i):
        return (x_any, all_x) if i == 0 else (g_any, all_g)

    def act_copies(i):
        source, target = act(i)
        place = target.at[me]
        return (
            remote(
                source.at[:, own_cut], target.at[me, :, own_cut],
                x_send.at[i], x_recv.at[i], "outer", across,
            ),
            remote(source, place, c_send.at[i], c_recv.at[i], "outer", sibling),
            pltpu.make_async_copy(source, place, own_sem.at[i]),
        )

    def term_copies(c):
        source = mine.at[c]
        place = terms.at[:, me, :, columns(c)]
        i = c + 2
        return (
            remote(source, place, x_send.at[i], x_recv.at[i], "outer", across),
            remote(source, place, c_send.at[i], c_recv.at[i], "outer", sibling),
            pltpu.make_async_copy(source, place, own_sem.at[i]),
        )

    def act_spread(i, d):
        place = act(i)[1].at[across, :, own_cut]
        return remote(place, place, z_send.at[i, d - 1], z_recv.at[i, d - 1], "mp", above(d))

    def act_forward(i):
        place = act(i)[1].at[across]
        return remote(place, place, f_send.at[i], f_recv.at[i], "outer", sibling)

    def term_forward(c):
        place = terms.at[:, across, :, columns(c)]
        return remote(place, place, f_send.at[c + 2], f_recv.at[c + 2], "outer", sibling)

    def back_scatter(d):
        return remote(
            back_out.at[above(d)], back_in.at[d - 1], s_send.at[d - 1], s_recv.at[d - 1], "mp", above(d)
        )

    def back_gather(d):
        place = back_all.at[level]
        return remote(place, place, g_send.at[d - 1], g_recv.at[d - 1], "mp", above(d))

    def y_copy(c):
        return remote(partial.at[c], other.at[c], y_send.at[c], y_recv.at[c], "dp", width)

    for i in range(2):
        for copy in act_copies(i):
            copy.start()
    acc[...] = jnp.zeros_like(acc)

    def step(s, carry):
        @pl.when(s < chunks)
        def _():
            for k in range(3):
                load(s, k).wait()
            x = x_ref[...]
            partial[s, 0] = mm(x, wg[s], ((1,), (0,))).astype(BF16)
            partial[s, 1] = mm(x, wu[s], ((1,), (0,))).astype(BF16)
            partial[s, 2] = mm(g_ref[...], wd[s], ((1,), (1,))).astype(BF16)
            y_copy(s).start()

            @pl.when(s + AHEAD < chunks)
            def _():
                start_loads(s + AHEAD, 0)

        @pl.when(s >= LAG)
        def _():
            c = s - LAG
            y_copy(c).wait_recv()
            gate, up, hidden_grad = [
                partial[c, k].astype(jnp.float32) + other[c, k].astype(jnp.float32) for k in range(3)
            ]
            hidden, gate_term, up_term = terms_of(gate, up, hidden_grad)
            mine[c, 0] = hidden
            mine[c, 1] = gate_term
            mine[c, 2] = up_term
            for copy in term_copies(c):
                copy.start()
            acc[...] += mm(gate_term, wg[c], ((1,), (1,))) + mm(up_term, wu[c], ((1,), (1,)))

        @pl.when(s == 2)
        def _():
            for i in range(2):
                act_copies(i)[0].wait_recv()
                for d in range(1, levels):
                    act_spread(i, d).start()

        return carry

    lax.fori_loop(0, chunks + LAG, step, 0)
    for j in range(levels):
        back_out[j] = acc[:, j * quarter:(j + 1) * quarter].astype(BF16)
    for d in range(1, levels):
        back_scatter(d).start()

    for i in range(2):
        for d in range(1, levels):
            act_spread(i, d).wait_recv()
        act_forward(i).start()

    def forward(c, carry):
        term_copies(c)[0].wait_recv()
        term_forward(c).start()
        return carry

    lax.fori_loop(0, chunks - 1, forward, 0)

    total = back_out[level].astype(jnp.float32)
    for d in range(1, levels):
        back_scatter(d).wait_recv()
        total = total + back_in[d - 1].astype(jnp.float32)
    back_all[level] = total.astype(BF16)
    for d in range(1, levels):
        back_gather(d).start()

    forward(chunks - 1, 0)

    for d in range(1, levels):
        back_gather(d).wait_recv()
    for j in range(levels):
        back[:, j * quarter:(j + 1) * quarter] = back_all[j]
    for d in range(1, levels):
        back_scatter(d).wait_send()
        back_gather(d).wait_send()

    def finish(copies, passed):
        copies[0].wait_send()
        copies[1].wait()
        copies[2].wait()
        passed.wait()

    for i in range(2):
        finish(act_copies(i), act_forward(i))
        for d in range(1, levels):
            act_spread(i, d).wait_send()

    def drain(c, carry):
        y_copy(c).wait_send()
        finish(term_copies(c), term_forward(c))
        return carry

    lax.fori_loop(0, chunks, drain, 0)


def exchange(levels, inputs, out_grad, w_gate, w_up, w_down):
    rows, width = inputs.shape
    quarter = width // levels
    hidden = w_gate.shape[1]
    chunks = hidden // CHUNK
    any_spec = pl.BlockSpec(memory_space=pl.ANY)
    vmem_spec = pl.BlockSpec(memory_space=pltpu.VMEM)
    dma = pltpu.SemaphoreType.DMA
    items = dma((chunks + 2,))
    return pl.pallas_call(
        functools.partial(exchange_kernel, chunks),
        out_shape=(
            jax.ShapeDtypeStruct((4, rows, width), BF16),
            jax.ShapeDtypeStruct((4, rows, width), BF16),
            jax.ShapeDtypeStruct((3, 4, rows, hidden), BF16),
            jax.ShapeDtypeStruct((rows, width), BF16),
        ),
        in_specs=[vmem_spec] * 2 + [any_spec] * 5,
        out_specs=(any_spec, any_spec, any_spec, vmem_spec),
        scratch_shapes=[
            pltpu.VMEM((chunks, width, CHUNK), BF16),
            pltpu.VMEM((chunks, width, CHUNK), BF16),
            pltpu.VMEM((chunks, CHUNK, width), BF16),
            pltpu.VMEM((chunks, 3, rows, CHUNK), BF16),
            pltpu.VMEM((chunks, 3, rows, CHUNK), BF16),
            pltpu.VMEM((chunks, 3, rows, CHUNK), BF16),
            pltpu.VMEM((rows, width), jnp.float32),
            pltpu.VMEM((levels, rows, quarter), BF16),
            pltpu.VMEM((levels - 1, rows, quarter), BF16),
            pltpu.VMEM((levels, rows, quarter), BF16),
            dma((3, chunks)), dma((chunks,)), dma((chunks,)),
            items, items, items, items, items, items, items,
            dma((2, levels - 1)), dma((2, levels - 1)),
            dma((levels - 1,)), dma((levels - 1,)), dma((levels - 1,)), dma((levels - 1,)),
        ],
        compiler_params=pltpu.CompilerParams(
            collective_id=0, has_side_effects=True, vmem_limit_bytes=60 * 1024 * 1024
        ),
    )(inputs, out_grad, inputs, out_grad, w_gate, w_up, w_down)


PARTS = 4


def grads_kernel(x_ref, g_ref, h_ref, gt_ref, ut_ref, back_ref, gate_out, up_out, down_out, back_out):
    @pl.when(pl.program_id(0) == 0)
    def _():
        back_out[...] = back_ref[...]

    left = x_ref[...].T
    for start in range(0, gate_out.shape[1], 1024):
        cut = slice(start, start + 1024)
        gate_out[:, cut] = jnp.dot(left, gt_ref[0, :, cut], preferred_element_type=jnp.float32).astype(BF16)
        up_out[:, cut] = jnp.dot(left, ut_ref[0, :, cut], preferred_element_type=jnp.float32).astype(BF16)
    left = h_ref[0].T
    for start in range(0, down_out.shape[1], 1024):
        cut = slice(start, start + 1024)
        down_out[:, cut] = jnp.dot(left, g_ref[:, cut], preferred_element_type=jnp.float32).astype(BF16)


def weight_grads(all_x, all_g, terms, back):
    tokens, width = all_x.shape
    hidden = terms.shape[2]
    cost = pl.CostEstimate(
        flops=6 * tokens * width * hidden,
        bytes_accessed=2 * (3 * width * hidden + tokens * (2 * width + 3 * hidden)),
        transcendentals=0,
    )
    return pl.pallas_call(
        grads_kernel,
        grid=(PARTS,),
        out_shape=(
            jax.ShapeDtypeStruct((width, hidden), BF16),
            jax.ShapeDtypeStruct((width, hidden), BF16),
            jax.ShapeDtypeStruct((hidden, width), BF16),
            jax.ShapeDtypeStruct(back.shape, BF16),
        ),
        in_specs=[
            pl.BlockSpec((tokens, width // PARTS), lambda i: (0, i)),
            pl.BlockSpec((tokens, width), lambda i: (0, 0)),
            pl.BlockSpec((1, tokens, hidden // PARTS), lambda i: (0, 0, i)),
            pl.BlockSpec((1, tokens, hidden), lambda i: (1, 0, 0)),
            pl.BlockSpec((1, tokens, hidden), lambda i: (2, 0, 0)),
            pl.BlockSpec(back.shape, lambda i: (0, 0)),
        ],
        out_specs=(
            pl.BlockSpec((width // PARTS, hidden), lambda i: (i, 0)),
            pl.BlockSpec((width // PARTS, hidden), lambda i: (i, 0)),
            pl.BlockSpec((hidden // PARTS, width), lambda i: (i, 0)),
            pl.BlockSpec(back.shape, lambda i: (0, 0)),
        ),
        compiler_params=pltpu.CompilerParams(vmem_limit_bytes=60 * 1024 * 1024),
        cost_estimate=cost,
    )(all_x, all_g, terms, terms, terms, back)


def on_device_kernels(levels, inputs, out_grad, w_gate, w_up, w_down):
    all_x, all_g, terms, back = exchange(levels, inputs, out_grad, w_gate, w_up, w_down)
    rows, width = inputs.shape
    hidden = w_gate.shape[1]
    gate_grad, up_grad, down_grad, input_grad = weight_grads(
        all_x.reshape(4 * rows, width), all_g.reshape(4 * rows, width), terms.reshape(3, 4 * rows, hidden), back
    )
    return input_grad, gate_grad, up_grad, down_grad


def solution(mesh):
    dp = mesh.shape["dp"]
    in_specs = (P("outer", "dp"), P("outer", "dp"), P("dp", "mp"), P("dp", "mp"), P("mp", "dp"))
    out_specs = (P("outer", "dp"), P("dp", "mp"), P("dp", "mp"), P("mp", "dp"))

    def body(*arrays):
        rows, width = arrays[0].shape
        hidden = arrays[2].shape[1]
        fits = rows % 16 == 0 and 6 * width * hidden <= 40 * 1024 * 1024
        tiles = width % 1024 == 0 and hidden % 1024 == 0
        if dp == 2 and mesh.shape["outer"] == 4 and mesh.shape["mp"] == 4 and fits and tiles:
            return on_device_kernels(mesh.shape["mp"], *arrays)
        return on_device(dp, *arrays)

    return jax.shard_map(body, mesh=mesh, in_specs=in_specs, out_specs=out_specs, check_vma=False)
```
